512 devices in a mesh: seq: 8 (over x, core), expert: 64 (over z, y).
Axes of the slice: x: 4, y: 8, z: 8, core: 2. Of those that a mesh axis runs over, the one named last changes fastest.
Arguments:
- dy_values: bfloat16 [64, 128, 4096], P('expert', None, 'seq'), may hold values from -6 to 6
- dy_scales: float32 [64, 128, 32], P('expert', None, 'seq'), may hold values from 0.3 to 3
- route_expert: int32 [64, 128, 8], P('expert'), may hold values from 0 to 63, all different within a row; in each aligned block of 128 rows (0 to 127, 128 to 255, ..., all dimensions but the last counted through in order) at most 20 rows name the same one
- gate_weight: float32 [64, 128, 8], P('expert'), may hold values from 0.05 to 0.5
- saved_pre: bfloat16 [64, 1280, 2, 1024], P('expert', 'seq'), may hold values from -6 to 6
- w_gate: bfloat16 [64, 4096, 1024], P('expert', 'seq'), may hold values from -0.09375 to 0.09375
- w_up: bfloat16 [64, 4096, 1024], P('expert', 'seq'), may hold values from -0.09375 to 0.09375
- w_down: bfloat16 [64, 1024, 4096], P('expert', None, 'seq'), may hold values from -0.1875 to 0.1875
- w_scale: float32 [3, 64, 32, 8], P(None, 'expert', 'seq'), may hold values from 0.5 to 2
Outputs:
- input_grad: bfloat16 [64, 128, 4096], P('expert', None, 'seq')
- down_grad: bfloat16 [64, 1024, 4096], P('expert', None, 'seq')
The draws below stay inside these ranges and needn't reach their ends.
Inputs may be any that keep to these rules, and one draw needn't show every extreme that they name: `route_expert`: each row names 8 different experts and every expert is named somewhere. Within one group no expert is named by more than 20 entries, and in every draw some expert is named by exactly 20 entries of some group.
All inputs are finite; a program needn't handle non-finite values.
Results may differ from the reference program's by a relative error of at most 0.023.
Values may be sent and summed in bfloat16 or wider, within the bound.
No kernel may reach another device: no remote copies, remote signals or barrier semaphores. Data moves between devices by JAX's collectives and lax.ppermute only.
A program may use at most 64 MiB of HBM per device.

```python
import math
import jax
import jax.numpy as jnp
import numpy as np
from jax import lax

D = 4096
H = 1024
QB = 128
TOPK = 8
GROUP_TOK = 128
EXPERTS = 64
GROUPS = 64
CAP = 20
N_SEQ = 8


def block_levels(key, dims, split, least, top_value):
    level, own = 1.0, jax.random.fold_in(key, 6)
    for dim, blocks in split:
        draws = jnp.exp(jax.random.uniform(jax.random.fold_in(own, dim), (blocks,), jnp.float32, least / len(split), top_value / len(split)))
        level = level * jnp.repeat(draws, dims[dim] // blocks).reshape([-1 if axis == dim else 1 for axis in range(len(dims))])
    return level


def routed_block(key, own, number, rows, number_of, top, bound, slope):
    sequence = jax.random.permutation(key, number_of)
    heavy_load, ordinary = shares(number_of, rows * top, bound, slope, True), shares(number_of, rows * top, bound, slope, False)
    places = jnp.arange(number_of)

    def named(tallies, offset_by):
        used = int((tallies > 0).sum())
        fixed = max(1, used // 4)
        shifted = fixed + (places - fixed + offset_by * (used - fixed)) % max(1, number_of - fixed)
        return jnp.zeros((number_of,), jnp.int32).at[sequence[jnp.where(places < fixed, places, shifted)]].set(jnp.asarray(tallies, jnp.int32))

    tallies = jnp.where(number % 4 == 0, named(heavy_load, number // 4), named(ordinary, number - number // 4 - 1))
    mixed = jax.random.permutation(jax.random.fold_in(own, 3), number_of)
    source_of, receiver = mixed[0:number_of // 2 * 2:2], mixed[1:number_of // 2 * 2:2]
    slack = jnp.minimum(tallies[source_of] - 1, bound - tallies[receiver]) // 2
    slack = jnp.where((source_of == sequence[0]) | (receiver == sequence[0]) | (tallies[receiver] == 0), 0, jnp.maximum(slack, 0))
    shifted = jax.random.randint(jax.random.fold_in(own, 4), (number_of // 2,), 0, 1 << 20) % (slack + 1)
    tallies = tallies.at[source_of].add(-shifted).at[receiver].add(shifted)
    items = jnp.searchsorted(jnp.cumsum(tallies), jnp.arange(rows * top), side="right").astype(jnp.int32)
    listing = items.reshape(top, rows).T
    listing = listing[jax.random.permutation(jax.random.fold_in(own, 1), rows)]
    offset_by = jax.random.randint(jax.random.fold_in(own, 2), (rows, 1), 0, top)
    return jnp.take_along_axis(listing, (jnp.arange(top)[None, :] + offset_by) % top, axis=1)


def shares(count, total, limit, lean, full):
    weights = [(1 << 20) // math.isqrt(rank ** lean) + 1 for rank in range(1, count + 1)]
    largest = limit if full else min(limit, max(-(-total // count), total * weights[0] // sum(weights)))
    least = 1 if total - largest >= count - 1 else 0
    holding, surplus = [largest] + [least] * (count - 1), total - largest - least * (count - 1)
    while surplus > 0:
        free = [i for i in range(1, count) if holding[i] < largest] or [i for i in range(1, count) if holding[i] < limit]
        whole, left = sum([weights[i] for i in free]), surplus
        for i in free:
            addition = min(limit - holding[i], max(1, left * weights[i] // whole), surplus)
            holding[i] = holding[i] + addition
            surplus = surplus - addition
    return np.array(holding)


def normal_values(rng, extent, scale, most, split=(), held_as=jnp.bfloat16):
    values = jax.random.normal(rng, extent, jnp.float32) * scale
    if len(split) > 0:
        values = block_levels(rng, extent, split, -0.22, 0.18) * values
    return jnp.clip(values, min=-most, max=most).astype(held_as)


def setup_inputs(seed: int = 0) -> dict:
    keys = jax.random.split(jax.random.key(seed), 10)
    dy_values = normal_values(keys[0], (GROUPS, GROUP_TOK, D), 1.0, 6.0, ((0, 64), (2, 8)))
    dy_scales = jnp.clip(jnp.exp(math.log(3.0) - 2.3025851 * jax.random.uniform(keys[1], (GROUPS, GROUP_TOK, D // QB), jnp.float32) ** block_levels(keys[1], (GROUPS, GROUP_TOK, D // QB), ((0, 64), (2, 8)), -0.2, 0.2)), 0.3, 3.0)
    route_expert_keys = jax.random.split(jax.random.fold_in(keys[2], 1), GROUPS * GROUP_TOK // GROUP_TOK)
    route_expert_turns = jax.random.permutation(jax.random.fold_in(keys[2], 3), GROUPS * GROUP_TOK // GROUP_TOK)
    route_expert = jax.vmap(lambda own, number: routed_block(jax.random.fold_in(keys[2], 2), own, number, GROUP_TOK, EXPERTS, TOPK, CAP, 2))(route_expert_keys, route_expert_turns).reshape((GROUPS, GROUP_TOK, TOPK))
    gate_weight = jnp.clip(0.05 + 0.45 * jax.random.uniform(keys[3], (GROUPS, GROUP_TOK, TOPK), jnp.float32) ** block_levels(keys[3], (GROUPS, GROUP_TOK, TOPK), ((0, 64),), -0.2, 0.2), 0.05, 0.5)
    saved_pre = normal_values(keys[4], (EXPERTS, GROUPS * CAP, 2, H), 1.5, 6.0, ((0, 64), (1, 8)))
    w_gate = normal_values(keys[5], (EXPERTS, D, H), D ** -0.5, 0.09375, ((0, 64), (1, 8)))
    w_up = normal_values(keys[6], (EXPERTS, D, H), D ** -0.5, 0.09375, ((0, 64), (1, 8)))
    w_down = normal_values(keys[7], (EXPERTS, H, D), H ** -0.5, 0.1875, ((0, 64), (2, 8)))
    w_scale = jnp.clip(jnp.exp(math.log(2.0) - 1.3862944 * jax.random.uniform(keys[8], (3, EXPERTS, D // QB, H // QB), jnp.float32) ** block_levels(keys[8], (3, EXPERTS, D // QB, H // QB), ((1, 64), (2, 8)), -0.2, 0.2)), 0.5, 2.0)
    return dict(dy_values=dy_values, dy_scales=dy_scales, route_expert=route_expert, gate_weight=gate_weight, saved_pre=saved_pre, w_gate=w_gate, w_up=w_up, w_down=w_down, w_scale=w_scale)


def dequant_rows(values, scales):
    lead = values.shape[:-1]
    blocks = scales.shape[-1]
    width = values.shape[-1]
    grid = values.astype(jnp.float32).reshape(lead + (blocks, width // blocks))
    return (grid * scales[..., None]).reshape(lead + (width,)).astype(jnp.bfloat16)


def dequant_matrix(values, scales):
    rows_in, cols_in = values.shape
    row_blocks, col_blocks = scales.shape
    grid = values.astype(jnp.float32).reshape(row_blocks, rows_in // row_blocks, col_blocks, cols_in // col_blocks)
    return (grid * scales[:, None, :, None]).reshape(rows_in, cols_in).astype(jnp.bfloat16)


def slot_table(routes, expert_count):
    labels = jnp.arange(expert_count, dtype=jnp.int32)
    onehot = (routes[:, :, None] == labels[None, None, :]).astype(jnp.int32)
    per_token = jnp.sum(onehot, axis=1)
    earlier = jnp.cumsum(per_token, axis=0) - per_token
    return jnp.sum(onehot * earlier[:, None, :], axis=2).astype(jnp.int32)


def selection(routes, weights, expert_count, cap_slots):
    slots = slot_table(routes, expert_count)
    target = routes * cap_slots + slots
    places = jnp.arange(expert_count * cap_slots, dtype=jnp.int32)
    match_all = target[None, :, :] == places[:, None, None]
    picked = jnp.sum(jnp.where(match_all, weights[None, :, :], jnp.zeros_like(weights)[None, :, :]), axis=2)
    plain = jnp.sum(match_all.astype(jnp.float32), axis=2)
    return picked, plain


def reference(dy_values, dy_scales, route_expert, gate_weight, saved_pre, w_gate, w_up, w_down, w_scale):
    rows_all = GROUPS * CAP
    cols_dev = D // N_SEQ
    dy_full = dequant_rows(dy_values, dy_scales)

    def dispatch_group(inputs):
        routes, weights, tokens = inputs
        picked, plain = selection(routes, weights, EXPERTS, CAP)
        sent = jnp.dot(picked, tokens.astype(jnp.float32), precision=lax.Precision.HIGHEST)
        return sent.astype(jnp.bfloat16)

    sent_all = lax.map(dispatch_group, (route_expert, gate_weight, dy_full))
    by_expert = jnp.swapaxes(sent_all.reshape(GROUPS, EXPERTS, CAP, D), 0, 1).reshape(EXPERTS, rows_all, D)

    def expert_step(inputs):
        rows, saved, gate_q, up_q, down_q, scales = inputs
        w_gate_eff = dequant_matrix(gate_q, scales[0])
        w_up_eff = dequant_matrix(up_q, scales[1])
        w_down_eff = dequant_matrix(down_q, scales[2].T)
        split_rows = rows.reshape(rows_all, N_SEQ, cols_dev).astype(jnp.float32)
        split_down = w_down_eff.reshape(H, N_SEQ, cols_dev).astype(jnp.float32)
        partial_value = jnp.einsum("rsk,hsk->srh", split_rows, split_down)
        rounded = lax.optimization_barrier(partial_value.astype(jnp.bfloat16)).astype(jnp.float32)
        hidden_grad = jnp.sum(rounded, axis=0)
        gate_pre = saved[:, 0, :].astype(jnp.float32)
        up_pre = saved[:, 1, :].astype(jnp.float32)
        gate_sig = jax.nn.sigmoid(gate_pre)
        silu_gate = gate_pre * gate_sig
        hidden_act = (silu_gate * up_pre).astype(jnp.bfloat16)
        up_grad = (hidden_grad * silu_gate).astype(jnp.bfloat16)
        gate_grad = (hidden_grad * up_pre * gate_sig * (1.0 + gate_pre * (1.0 - gate_sig))).astype(jnp.bfloat16)
        contract = (((1,), (1,)), ((), ()))
        input_rows = lax.dot_general(gate_grad, w_gate_eff, contract, preferred_element_type=jnp.float32)
        input_rows = input_rows + lax.dot_general(up_grad, w_up_eff, contract, preferred_element_type=jnp.float32)
        weight_grad = lax.dot_general(hidden_act, rows, (((0,), (0,)), ((), ())), preferred_element_type=jnp.float32)
        return input_rows.astype(jnp.bfloat16), weight_grad.astype(jnp.bfloat16)

    scale_by_expert = jnp.swapaxes(w_scale, 0, 1)
    expert_rows, down_grad = lax.map(expert_step, (by_expert, saved_pre, w_gate, w_up, w_down, scale_by_expert))
    by_group = jnp.swapaxes(expert_rows.reshape(EXPERTS, GROUPS, CAP, D), 0, 1).reshape(GROUPS, EXPERTS * CAP, D)

    def combine_group(inputs):
        routes, weights, returned = inputs
        picked, plain = selection(routes, weights, EXPERTS, CAP)
        summed = jnp.dot(plain.T.astype(jnp.bfloat16), returned, preferred_element_type=jnp.float32)
        return summed.astype(jnp.bfloat16)

    input_grad = lax.map(combine_group, (route_expert, gate_weight, by_group))
    return input_grad, down_grad
```

```python
import functools

import jax
import jax.numpy as jnp
from jax import lax
from jax.experimental import pallas as pl
from jax.experimental.pallas import tpu as pltpu
from jax.sharding import Mesh
from jax.sharding import PartitionSpec as P

EXPERT = ("z", "y")
XS = 4
CHUNKS = 2
HIGHEST = lax.Precision.HIGHEST
NT = (((1,), (1,)), ((), ()))
TN = (((0,), (0,)), ((), ()))
F32 = jnp.float32
BF16 = jnp.bfloat16


def vmem_call(body, out_shape, n_smem, n_in, flops, nbytes, scratch=(), limit=40 << 20):
    smem = pl.BlockSpec(memory_space=pltpu.SMEM)
    vmem = pl.BlockSpec(memory_space=pltpu.VMEM)
    outs = jax.tree.map(lambda _: vmem, out_shape)
    return pl.pallas_call(
        body,
        out_shape=out_shape,
        in_specs=[smem] * n_smem + [vmem] * n_in,
        out_specs=outs,
        scratch_shapes=list(scratch),
        compiler_params=pltpu.CompilerParams(vmem_limit_bytes=limit),
        cost_estimate=pl.CostEstimate(flops=flops, bytes_accessed=nbytes, transcendentals=0),
    )


def dequant_rows(values, scales):
    lead = values.shape[:-1]
    blocks = scales.shape[-1]
    width = values.shape[-1]
    grid = values.astype(F32).reshape(lead + (blocks, width // blocks))
    return (grid * scales[..., None]).reshape(lead + (width,)).astype(BF16)


def dequant_matrix(values, scales):
    rows_in, cols_in = values.shape
    row_blocks, col_blocks = scales.shape
    grid = values.astype(F32).reshape(
        row_blocks, rows_in // row_blocks, col_blocks, cols_in // col_blocks
    )
    return (grid * scales[:, None, :, None]).reshape(rows_in, cols_in).astype(BF16)


def select_body(experts, slots, core_ref, route_ref, weight_ref, pick_ref, gate_ref):
    top, tokens = route_ref.shape
    rows = experts * slots
    label = lax.broadcasted_iota(jnp.int32, (experts, tokens), 0)
    named = jnp.zeros((experts, tokens), F32)
    weight = jnp.zeros((experts, tokens), F32)
    for k in range(top):
        hit = route_ref[k : k + 1, :] == label
        named = named + jnp.where(hit, 1.0, 0.0)
        weight = weight + jnp.where(hit, weight_ref[k : k + 1, :], 0.0)
    before = lax.broadcasted_iota(jnp.int32, (tokens, tokens), 0) < lax.broadcasted_iota(
        jnp.int32, (tokens, tokens), 1
    )
    earlier = jnp.dot(
        named.astype(BF16), jnp.where(before, 1.0, 0.0).astype(BF16), preferred_element_type=F32
    )
    slot = jnp.where(named > 0.0, earlier, -1.0)
    row = lax.broadcasted_iota(jnp.int32, (rows, experts), 0)
    first = lax.broadcasted_iota(jnp.int32, (rows, experts), 1) * slots
    spread = jnp.where((row >= first) & (row < first + slots), 1.0, 0.0)
    slot_row = jnp.dot(spread.astype(BF16), slot.astype(BF16), preferred_element_type=F32)
    weight_row = jnp.dot(spread, weight, precision=HIGHEST, preferred_element_type=F32)
    place = lax.broadcasted_iota(jnp.int32, (rows, tokens), 0).astype(F32)
    place = place - slots * jnp.floor((place + 0.5) * (1.0 / slots))
    base = (core_ref[0] * (slots * CHUNKS)).astype(F32)
    for ch in range(CHUNKS):
        hit = slot_row == place + (base + float(ch * slots))
        pick_ref[ch] = jnp.where(hit, 1.0, 0.0).astype(BF16)
        gate = jnp.sum(jnp.where(hit, weight_row, 0.0), axis=1, keepdims=True)
        gate_ref[ch] = jnp.broadcast_to(gate, (rows, tokens))


def dispatch_body(pick_ref, gate_ref, mine_ref, other_ref, *out_refs):
    half = mine_ref.shape[1]
    for ch in range(CHUNKS):
        pick = pick_ref[ch]
        gate = gate_ref[ch][:, :1]
        out = out_refs[ch]
        out[:, :half] = (jnp.dot(pick, mine_ref[...], preferred_element_type=F32) * gate).astype(BF16)
        out[:, half:] = (jnp.dot(pick, other_ref[...], preferred_element_type=F32) * gate).astype(BF16)


def hidden_body(x_ref, rows_ref, mine_ref, other_ref, own_ref, *send_refs):
    half = mine_ref.shape[1]
    size = own_ref.shape[0]
    for k in range(XS):
        at = pl.multiple_of(lax.rem(x_ref[0] + k, XS) * size, 16)
        rows = rows_ref[pl.ds(at, size), :]
        part = lax.dot_general(rows[:, :half], mine_ref[...], NT, preferred_element_type=F32)
        part = part + lax.dot_general(rows[:, half:], other_ref[...], NT, preferred_element_type=F32)
        if k == 0:
            own_ref[...] = part
        else:
            send_refs[k - 1][...] = part.astype(BF16)


def back_body(x_ref, h0, h1, h2, h3, fac_ref, gm_ref, go_ref, um_ref, uo_ref, out_ref, gate_s, up_s):
    size = h0.shape[0]
    half = gm_ref.shape[0]
    for k, h in enumerate((h0, h1, h2, h3)):
        block = lax.rem(x_ref[0] + (XS - k), XS)
        at = pl.multiple_of(block * size, 16)
        grad = h[...].astype(F32)
        up_s[pl.ds(at, size), :] = (grad * fac_ref[block, 0].astype(F32)).astype(BF16)
        gate_s[pl.ds(at, size), :] = (grad * fac_ref[block, 1].astype(F32)).astype(BF16)
    for lo, g, u in ((0, gm_ref, um_ref), (half, go_ref, uo_ref)):
        total = lax.dot_general(gate_s[...], g[...], NT, preferred_element_type=F32)
        total = total + lax.dot_general(up_s[...], u[...], NT, preferred_element_type=F32)
        out_ref[:, lo : lo + half] = total.astype(BF16)


def swap(value):
    return lax.ppermute(value, "core", [(0, 1), (1, 0)])


def shift(value, k):
    return lax.ppermute(value, "x", [(i, (i + k) % XS) for i in range(XS)])


def shards(
    dy_values, dy_scales, route_expert, gate_weight, saved_pre, w_gate, w_up, w_down, w_scale
):
    core = lax.axis_index("core").astype(jnp.int32)
    xpos = lax.axis_index("x").astype(jnp.int32)[None]
    experts = lax.axis_size(EXPERT)
    tokens, cols = dy_values.shape[1:]
    rows_dev, _, hid = saved_pre.shape[1:]
    width = 2 * cols
    cap = rows_dev * XS * 2 // experts
    slots = cap // 2 // CHUNKS
    rows = experts * slots
    size = rows // XS

    mine = dequant_rows(dy_values[0], dy_scales[0])
    other = swap(mine)
    pick, gate = vmem_call(
        functools.partial(select_body, experts, slots),
        (
            jax.ShapeDtypeStruct((CHUNKS, rows, tokens), BF16),
            jax.ShapeDtypeStruct((CHUNKS, rows, tokens), F32),
        ),
        1, 2, 4 * rows * experts * tokens, 4 << 20,
    )(core[None], route_expert[0].T, gate_weight[0].T)
    outgoing = vmem_call(
        dispatch_body,
        tuple(jax.ShapeDtypeStruct((rows, width), BF16) for _ in range(CHUNKS)),
        0, 4, 2 * CHUNKS * rows * tokens * width, 4 << 20,
    )(pick, gate, mine, other)
    block = (experts, slots * width // 128, 128)
    incoming = []
    for ch in range(CHUNKS):
        got = lax.all_to_all(outgoing[ch].reshape(block), EXPERT, 0, 0, tiled=True)
        incoming.append(got.reshape(rows, width))

    pre = saved_pre[0]
    gate_pre = pre[:, 0, :].astype(F32)
    up_pre = pre[:, 1, :].astype(F32)
    sig = jax.nn.sigmoid(gate_pre)
    silu = gate_pre * sig
    factors = jnp.stack(
        [
            silu.astype(BF16),
            (up_pre * sig * (1.0 + gate_pre * (1.0 - sig))).astype(BF16),
            (silu * up_pre).astype(BF16),
        ]
    )
    groups = rows_dev // cap
    factors = factors.reshape(3, groups, 2, CHUNKS, slots, hid).transpose(2, 0, 3, 1, 4, 5)
    factors = factors.reshape(2, 3, CHUNKS, groups * slots, hid)
    kept = lax.dynamic_index_in_dim(factors, core, 0, keepdims=False)
    came = swap(lax.dynamic_index_in_dim(factors, 1 - core, 0, keepdims=False))
    low = jnp.where(core == 0, kept, came)
    high = jnp.where(core == 0, came, kept)
    factors = jnp.concatenate([low, high], axis=2)
    factors = lax.all_gather(factors, "x", axis=0, tiled=False)

    scales = w_scale[:, 0]
    gate_m = dequant_matrix(w_gate[0], scales[0])
    up_m = dequant_matrix(w_up[0], scales[1])
    down_m = dequant_matrix(w_down[0], scales[2].T)
    down_o = swap(down_m)
    gate_o = swap(gate_m)
    up_o = swap(up_m)

    sent = []
    for ch in range(CHUNKS):
        parts = vmem_call(
            hidden_body,
            (jax.ShapeDtypeStruct((size, hid), F32),)
            + tuple(jax.ShapeDtypeStruct((size, hid), BF16) for _ in range(XS - 1)),
            1, 3, 2 * rows * width * hid, 6 << 20,
        )(xpos, incoming[ch], down_m, down_o)
        total = parts[0]
        for k in (1, 3, 2):
            total = total + shift(parts[k], k).astype(F32)
        grad = total.astype(BF16)
        grads = [grad] + [shift(grad, k) for k in (1, 2, 3)]
        value = vmem_call(
            back_body,
            jax.ShapeDtypeStruct((rows, width), BF16),
            1, 9, 4 * rows * width * hid, 8 << 20,
            scratch=(pltpu.VMEM((rows, hid), BF16), pltpu.VMEM((rows, hid), BF16)),
        )(xpos, *grads, factors[:, :, ch], gate_m, gate_o, up_m, up_o)
        sent.append(lax.all_to_all(value.reshape(block), EXPERT, 0, 0, tiled=True))

    down_total = 0.0
    for ch in range(CHUNKS):
        act = factors[:, 2, ch].reshape(rows, hid)
        down_total = down_total + lax.dot_general(
            act, incoming[ch], TN, preferred_element_type=F32
        )
    down_grad = down_total[:, :cols] + swap(down_total[:, cols:].astype(BF16)).astype(F32)

    combined = 0.0
    for ch in range(CHUNKS):
        combined = combined + lax.dot_general(
            pick[ch], sent[ch].reshape(rows, width), TN, preferred_element_type=F32
        )
    input_grad = combined[:, :cols] + swap(combined[:, cols:])
    return (input_grad.astype(BF16)[None], down_grad.astype(BF16)[None])


def solution(mesh):
    devices = mesh.devices.reshape(XS, 2, 8, 8)
    fine = Mesh(devices, ("x", "core", "z", "y"))
    seq = ("x", "core")
    in_specs = (
        P(EXPERT, None, seq),
        P(EXPERT, None, seq),
        P(EXPERT, None, None),
        P(EXPERT, None, None),
        P(EXPERT, seq, None, None),
        P(EXPERT, seq, None),
        P(EXPERT, seq, None),
        P(EXPERT, None, seq),
        P(None, EXPERT, seq, None),
    )
    out_specs = (P(EXPERT, None, seq), P(EXPERT, None, seq))
    return jax.shard_map(shards, mesh=fine, in_specs=in_specs, out_specs=out_specs, check_vma=False)
```

```python
import functools

import jax
import jax.numpy as jnp
from jax import lax
from jax.experimental import pallas as pl
from jax.experimental.pallas import tpu as pltpu
from jax.sharding import Mesh
from jax.sharding import PartitionSpec as P

EXPERT = ("z", "y")
SEQ = ("x", "core")
XS = 4
CHUNKS = 1
LANES = 128
HIGHEST = lax.Precision.HIGHEST
NT = (((1,), (1,)), ((), ()))
TN = (((0,), (0,)), ((), ()))
F32 = jnp.float32
BF16 = jnp.bfloat16


def vmem_call(body, out_shape, n_smem, n_in, flops, nbytes, scratch=(), limit=40 << 20):
    smem = pl.BlockSpec(memory_space=pltpu.SMEM)
    vmem = pl.BlockSpec(memory_space=pltpu.VMEM)
    outs = jax.tree.map(lambda _: vmem, out_shape)
    return pl.pallas_call(
        body,
        out_shape=out_shape,
        in_specs=[smem] * n_smem + [vmem] * n_in,
        out_specs=outs,
        scratch_shapes=list(scratch),
        compiler_params=pltpu.CompilerParams(vmem_limit_bytes=limit),
        cost_estimate=pl.CostEstimate(flops=flops, bytes_accessed=nbytes, transcendentals=0),
    )


def shape(dims, dtype=BF16):
    return jax.ShapeDtypeStruct(dims, dtype)


def dequant_matrix(values, scales):
    rows_in, cols_in = values.shape
    row_blocks, col_blocks = scales.shape
    grid = values.astype(F32).reshape(
        row_blocks, rows_in // row_blocks, col_blocks, cols_in // col_blocks
    )
    return (grid * scales[:, None, :, None]).reshape(rows_in, cols_in).astype(BF16)


def iota(dims, axis):
    return lax.broadcasted_iota(jnp.int32, dims, axis)


def onehot(condition, dtype=BF16):
    return jnp.where(condition, 1.0, 0.0).astype(dtype)


def dy_body(value_ref, scale_ref, out_ref):
    blocks, cols = scale_ref.shape[0], value_ref.shape[1]
    first = iota((blocks, cols), 0) * (cols // blocks)
    lane = iota((blocks, cols), 1)
    spread = onehot((lane >= first) & (lane < first + cols // blocks), F32)
    scale = lax.dot_general(
        scale_ref[...], spread, TN, precision=HIGHEST, preferred_element_type=F32
    )
    out_ref[...] = (value_ref[...].astype(F32) * scale).astype(BF16)


def select_body(experts, slots, core_ref, route_ref, weight_ref, pick_ref, gate_ref):
    top, tokens = route_ref.shape
    rows = experts * slots
    label = iota((experts, tokens), 0)
    named = jnp.zeros((experts, tokens), F32)
    weight = jnp.zeros((experts, tokens), F32)
    for k in range(top):
        hit = route_ref[k : k + 1, :] == label
        named = named + jnp.where(hit, 1.0, 0.0)
        weight = weight + jnp.where(hit, weight_ref[k : k + 1, :], 0.0)
    before = onehot(iota((tokens, tokens), 0) < iota((tokens, tokens), 1))
    earlier = jnp.dot(named.astype(BF16), before, preferred_element_type=F32)
    slot = jnp.where(named > 0.0, earlier, -1.0)
    row = iota((rows, experts), 0)
    first = iota((rows, experts), 1) * slots
    spread = (row >= first) & (row < first + slots)
    slot_row = jnp.dot(onehot(spread), slot.astype(BF16), preferred_element_type=F32)
    weight_row = jnp.dot(
        onehot(spread, F32), weight, precision=HIGHEST, preferred_element_type=F32
    )
    place = iota((rows, tokens), 0).astype(F32)
    place = place - slots * jnp.floor((place + 0.5) * (1.0 / slots))
    base = (core_ref[0] * (slots * CHUNKS)).astype(F32)
    for ch in range(CHUNKS):
        hit = slot_row == place + (base + float(ch * slots))
        pick_ref[ch] = onehot(hit)
        gate = jnp.sum(jnp.where(hit, weight_row, 0.0), axis=1, keepdims=True)
        gate_ref[ch] = jnp.broadcast_to(gate, (rows, tokens))


def tile_rows(value, tile_s, at):
    rows = value.shape[0]
    per = tile_s.shape[0] // rows
    for j in range(value.shape[1] // LANES):
        tile_s[pl.ds(at + j, rows, stride=per), :] = value[:, j * LANES : (j + 1) * LANES]


def untile_rows(tile_ref, tile_s, rows_ref):
    rows, per = tile_ref.shape[:2]
    tile_s[...] = tile_ref[...].astype(F32).reshape(rows * per, LANES)
    for j in range(per):
        rows_ref[:, j * LANES : (j + 1) * LANES] = tile_s[pl.ds(j, rows, stride=per), :].astype(
            BF16
        )


def dispatch_body(pick_ref, gate_ref, mine_ref, other_ref, *refs):
    out_refs, tile_s = refs[:-1], refs[-1]
    for ch in range(CHUNKS):
        pick = pick_ref[ch]
        gate = gate_ref[ch][:, :1]
        for i, half in enumerate((mine_ref, other_ref)):
            rows = jnp.dot(pick, half[...], preferred_element_type=F32) * gate
            tile_rows(rows, tile_s, i * half.shape[1] // LANES)
        out_refs[ch][...] = tile_s[...].reshape(out_refs[ch].shape).astype(BF16)


def factor_body(slots, ch, core_ref, pre_ref, silu_ref, slope_ref, act_ref):
    rows, whole = silu_ref.shape[0], pre_ref.shape[1]
    cap = whole // (rows // slots)
    row = iota((rows, whole), 0).astype(F32)
    group = jnp.floor((row + 0.5) * (1.0 / slots))
    base = (core_ref[0] * (slots * CHUNKS) + ch * slots).astype(F32)
    pick = onehot(iota((rows, whole), 1).astype(F32) == row + group * (cap - slots) + base)
    gate_pre = jnp.dot(pick, pre_ref[0], preferred_element_type=F32)
    up_pre = jnp.dot(pick, pre_ref[1], preferred_element_type=F32)
    sig = jax.nn.sigmoid(gate_pre)
    silu = gate_pre * sig
    silu_ref[...] = silu.astype(BF16)
    slope_ref[...] = (up_pre * sig * (1.0 + gate_pre * (1.0 - sig))).astype(BF16)
    act_ref[...] = (silu * up_pre).astype(BF16)


def hidden_body(tile_ref, mine_ref, other_ref, rows_ref, low_ref, high_ref, tile_s):
    half = mine_ref.shape[1]
    size = low_ref.shape[0]
    untile_rows(tile_ref, tile_s, rows_ref)
    for i, out in enumerate((low_ref, high_ref)):
        rows = rows_ref[i * size : (i + 1) * size, :]
        part = lax.dot_general(rows[:, :half], mine_ref[...], NT, preferred_element_type=F32)
        part = part + lax.dot_general(
            rows[:, half:], other_ref[...], NT, preferred_element_type=F32
        )
        out[...] = part.astype(BF16)


def back_body(
    low, low_in, high, high_in, silu_ref, slope_ref, gm_ref, go_ref, um_ref, uo_ref,
    out_ref, gate_s, up_s, tile_s,
):
    size = low.shape[0]
    half = gm_ref.shape[0]
    for i, (here, came) in enumerate(((low, low_in), (high, high_in))):
        at = slice(i * size, (i + 1) * size)
        grad = here[...].astype(F32) + came[...].astype(F32)
        up_s[at, :] = (grad * silu_ref[at, :].astype(F32)).astype(BF16)
        gate_s[at, :] = (grad * slope_ref[at, :].astype(F32)).astype(BF16)
    for i, (g, u) in enumerate(((gm_ref, um_ref), (go_ref, uo_ref))):
        total = lax.dot_general(gate_s[...], g[...], NT, preferred_element_type=F32)
        total = total + lax.dot_general(up_s[...], u[...], NT, preferred_element_type=F32)
        tile_rows(total, tile_s, i * half // LANES)
    out_ref[...] = tile_s[...].reshape(out_ref.shape).astype(BF16)


def combine_body(pick_ref, tile_ref, out_ref, rows_s, tile_s):
    untile_rows(tile_ref, tile_s, rows_s)
    out_ref[...] = lax.dot_general(pick_ref[...], rows_s[...], TN, preferred_element_type=F32)


def swap(value):
    return lax.ppermute(value, "core", [(0, 1), (1, 0)])


def pair(value, mask):
    return lax.ppermute(value, "x", [(i, i ^ mask) for i in range(XS)])


def added(a, b):
    return (a.astype(F32) + b.astype(F32)).astype(BF16)


def shards(
    dy_values, dy_scales, route_expert, gate_weight, saved_pre, w_gate, w_up, w_down, w_scale
):
    core = lax.axis_index("core").astype(jnp.int32)[None]
    experts = lax.axis_size(EXPERT)
    tokens, cols = dy_values.shape[1:]
    rows_dev, _, hid = saved_pre.shape[1:]
    width = 2 * cols
    per = width // LANES
    cap = rows_dev * XS * 2 // experts
    slots = cap // 2 // CHUNKS
    rows = experts * slots
    tiles = (rows, per, LANES)
    block = (experts, slots * per, LANES)

    mine = vmem_call(dy_body, shape((tokens, cols)), 0, 2, 1 << 20, 1 << 18)(
        dy_values[0], dy_scales[0].T
    )
    other = swap(mine)
    pick, gate = vmem_call(
        functools.partial(select_body, experts, slots),
        (shape((CHUNKS, rows, tokens)), shape((CHUNKS, rows, tokens), F32)),
        1, 2, 4 * rows * experts * tokens, 1 << 20,
    )(core, route_expert[0].T, gate_weight[0].T)
    outgoing = vmem_call(
        dispatch_body,
        tuple(shape(tiles) for _ in range(CHUNKS)),
        0, 4, 2 * CHUNKS * rows * tokens * width, 2 << 20,
        scratch=(pltpu.VMEM((rows * per, LANES), F32),),
    )(pick, gate, mine, other)
    incoming = [
        lax.all_to_all(sent.reshape(block), EXPERT, 0, 0, tiled=True).reshape(tiles)
        for sent in outgoing
    ]

    saved_pre, w_gate, w_up, w_down, w_scale, _ = lax.optimization_barrier(
        (saved_pre, w_gate, w_up, w_down, w_scale, outgoing[0])
    )
    pre = lax.all_gather(saved_pre[0].transpose(1, 0, 2), SEQ, axis=1, tiled=True)
    scales = w_scale[:, 0]
    down_m = dequant_matrix(w_down[0], scales[2].T)
    gate_m = dequant_matrix(w_gate[0], scales[0])
    up_m = dequant_matrix(w_up[0], scales[1])
    down_o = swap(down_m)
    gate_o = swap(gate_m)
    up_o = swap(up_m)

    taken, returned, acts = [], [], []
    for ch in range(CHUNKS):
        silu, slope, act = vmem_call(
            functools.partial(factor_body, slots, ch),
            tuple(shape((rows, hid)) for _ in range(3)),
            1, 1, 4 * rows * rows_dev * XS * 2 * hid, 8 << 20,
        )(core, pre)
        acts.append(act)
        arrived, low, high = vmem_call(
            hidden_body,
            (shape((rows, width)), shape((rows // 2, hid)), shape((rows // 2, hid))),
            0, 3, 2 * rows * width * hid, 4 << 20,
            scratch=(pltpu.VMEM((rows * per, LANES), F32),),
        )(incoming[ch], down_m, down_o)
        taken.append(arrived)
        low = added(low, pair(low, 1))
        high = added(high, pair(high, 3))
        low_in = pair(low, 3)
        high_in = pair(high, 1)
        value = vmem_call(
            back_body,
            shape(tiles),
            0, 10, 4 * rows * width * hid, 6 << 20,
            scratch=(
                pltpu.VMEM((rows, hid), BF16),
                pltpu.VMEM((rows, hid), BF16),
                pltpu.VMEM((rows * per, LANES), F32),
            ),
        )(low, low_in, high, high_in, silu, slope, gate_m, gate_o, up_m, up_o)
        returned.append(
            lax.all_to_all(value.reshape(block), EXPERT, 0, 0, tiled=True).reshape(tiles)
        )

    down_total = 0.0
    for act, arrived in zip(acts, taken):
        down_total = down_total + lax.dot_general(act, arrived, TN, preferred_element_type=F32)
    down_grad = down_total[:, :cols] + swap(down_total[:, cols:].astype(BF16)).astype(F32)
    down_grad = down_grad.astype(BF16)[None]
    down_grad, *returned = lax.optimization_barrier((down_grad, *returned))

    combined = 0.0
    for ch in range(CHUNKS):
        combined = combined + vmem_call(
            combine_body,
            shape((tokens, width), F32),
            0, 2, 2 * rows * tokens * width, 2 << 20,
            scratch=(pltpu.VMEM((rows, width), BF16), pltpu.VMEM((rows * per, LANES), F32)),
        )(pick[ch], returned[ch])
    input_grad = combined[:, :cols] + swap(combined[:, cols:])
    return (input_grad.astype(BF16)[None], down_grad)


def solution(mesh):
    fine = Mesh(mesh.devices.reshape(XS, 2, 8, 8), SEQ + EXPERT)
    in_specs = (
        P(EXPERT, None, SEQ),
        P(EXPERT, None, SEQ),
        P(EXPERT, None, None),
        P(EXPERT, None, None),
        P(EXPERT, SEQ, None, None),
        P(EXPERT, SEQ, None),
        P(EXPERT, SEQ, None),
        P(EXPERT, None, SEQ),
        P(None, EXPERT, SEQ, None),
    )
    out_specs = (P(EXPERT, None, SEQ), P(EXPERT, None, SEQ))
    return jax.shard_map(shards, mesh=fine, in_specs=in_specs, out_specs=out_specs, check_vma=False)
```

```python
import functools

import jax
import jax.numpy as jnp
from jax import lax
from jax.experimental import pallas as pl
from jax.experimental.layout import Layout, with_layout_constraint
from jax.experimental.pallas import tpu as pltpu
from jax.sharding import Mesh
from jax.sharding import PartitionSpec as P

EXPERT = ("z", "y")
SEQ = ("x", "core")
XS = 4
LANES = 128
HIGHEST = lax.Precision.HIGHEST
NT = (((1,), (1,)), ((), ()))
TN = (((0,), (0,)), ((), ()))
F32 = jnp.float32
BF16 = jnp.bfloat16


def vmem_call(body, out_shape, n_smem, n_in, flops, nbytes, scratch=(), limit=16 << 20):
    smem = pl.BlockSpec(memory_space=pltpu.SMEM)
    vmem = pl.BlockSpec(memory_space=pltpu.VMEM)
    outs = jax.tree.map(lambda _: vmem, out_shape)
    return pl.pallas_call(
        body,
        out_shape=out_shape,
        in_specs=[smem] * n_smem + [vmem] * n_in,
        out_specs=outs,
        scratch_shapes=list(scratch),
        compiler_params=pltpu.CompilerParams(vmem_limit_bytes=limit),
        cost_estimate=pl.CostEstimate(flops=flops, bytes_accessed=nbytes, transcendentals=0),
    )


def shape(dims, dtype=BF16):
    return jax.ShapeDtypeStruct(dims, dtype)


def dequant_matrix(values, scales):
    rows_in, cols_in = values.shape
    row_blocks, col_blocks = scales.shape
    grid = values.astype(F32).reshape(
        row_blocks, rows_in // row_blocks, col_blocks, cols_in // col_blocks
    )
    return (grid * scales[:, None, :, None]).reshape(rows_in, cols_in).astype(BF16)


def iota(dims, axis):
    return lax.broadcasted_iota(jnp.int32, dims, axis)


def onehot(condition, dtype=BF16):
    return jnp.where(condition, 1.0, 0.0).astype(dtype)


def dy_body(value_ref, scale_ref, out_ref):
    blocks, cols = scale_ref.shape[0], value_ref.shape[1]
    first = iota((blocks, cols), 0) * (cols // blocks)
    lane = iota((blocks, cols), 1)
    spread = onehot((lane >= first) & (lane < first + cols // blocks), F32)
    scale = lax.dot_general(
        scale_ref[...], spread, TN, precision=HIGHEST, preferred_element_type=F32
    )
    out_ref[...] = (value_ref[...].astype(F32) * scale).astype(BF16)


def select_body(experts, slots, core_ref, route_ref, weight_ref, pick_ref, gate_ref):
    top, tokens = route_ref.shape
    rows = experts * slots
    label = iota((experts, tokens), 0)
    named = jnp.zeros((experts, tokens), F32)
    weight = jnp.zeros((experts, tokens), F32)
    for k in range(top):
        hit = route_ref[k : k + 1, :] == label
        named = named + jnp.where(hit, 1.0, 0.0)
        weight = weight + jnp.where(hit, weight_ref[k : k + 1, :], 0.0)
    before = onehot(iota((tokens, tokens), 0) < iota((tokens, tokens), 1))
    earlier = jnp.dot(named.astype(BF16), before, preferred_element_type=F32)
    slot = jnp.where(named > 0.0, earlier, -1.0)
    row = iota((rows, experts), 0)
    first = iota((rows, experts), 1) * slots
    spread = (row >= first) & (row < first + slots)
    slot_row = jnp.dot(onehot(spread), slot.astype(BF16), preferred_element_type=F32)
    weight_row = jnp.dot(
        onehot(spread, F32), weight, precision=HIGHEST, preferred_element_type=F32
    )
    place = iota((rows, tokens), 0).astype(F32)
    place = place - slots * jnp.floor((place + 0.5) * (1.0 / slots))
    hit = slot_row == place + (core_ref[0] * slots).astype(F32)
    pick_ref[...] = onehot(hit)
    gate = jnp.sum(jnp.where(hit, weight_row, 0.0), axis=1, keepdims=True)
    gate_ref[...] = jnp.broadcast_to(gate, (rows, tokens))


def tile_rows(value, tile_s, at):
    rows = value.shape[0]
    per = tile_s.shape[0] // rows
    for j in range(value.shape[1] // LANES):
        tile_s[pl.ds(at + j, rows, stride=per), :] = value[:, j * LANES : (j + 1) * LANES]


def untile_rows(tile_ref, tile_s, rows_ref):
    rows, per = tile_ref.shape[:2]
    tile_s[...] = tile_ref[...].astype(F32).reshape(rows * per, LANES)
    for j in range(per):
        rows_ref[:, j * LANES : (j + 1) * LANES] = tile_s[pl.ds(j, rows, stride=per), :].astype(
            BF16
        )


def dispatch_body(pick_ref, gate_ref, mine_ref, other_ref, out_ref, tile_s):
    pick = pick_ref[...]
    gate = gate_ref[:, :1]
    for i, half in enumerate((mine_ref, other_ref)):
        rows = jnp.dot(pick, half[...], preferred_element_type=F32) * gate
        tile_rows(rows, tile_s, i * half.shape[1] // LANES)
    out_ref[...] = tile_s[...].reshape(out_ref.shape).astype(BF16)


def side_body(turn, core_ref, pre_ref, rows_ref, *refs):
    outs, (silu_v, slope_v, act_v, mine_v, other_v, sems) = refs[-10:-6], refs[-6:]
    rows = rows_ref.shape[0]
    cols = mine_v.shape[1]
    size = rows // 4

    @pl.when(core_ref[0] == turn)
    def _():
        for at in range(0, rows, size):
            cut = slice(at, at + size)
            gate_pre = pre_ref[0, cut, :].astype(F32)
            up_pre = pre_ref[1, cut, :].astype(F32)
            sig = jax.nn.sigmoid(gate_pre)
            silu = gate_pre * sig
            silu_v[cut, :] = silu.astype(BF16)
            slope_v[cut, :] = (up_pre * sig * (1.0 + gate_pre * (1.0 - sig))).astype(BF16)
            act_v[cut, :] = (silu * up_pre).astype(BF16)
        held = (silu_v, slope_v, mine_v, other_v)
        stores = [
            pltpu.make_async_copy(src, dst, sems.at[i])
            for i, (src, dst) in enumerate(zip(held, outs))
        ]
        stores[0].start()
        stores[1].start()
        mine_v[...] = lax.dot_general(
            act_v[...], rows_ref[:, :cols], TN, preferred_element_type=F32
        )
        stores[2].start()
        other_v[...] = lax.dot_general(
            act_v[...], rows_ref[:, cols:], TN, preferred_element_type=F32
        ).astype(BF16)
        stores[3].start()
        for store in stores:
            store.wait()


def side_call(turn, core, pre, arrived, before):
    rows, width = arrived.shape
    hid = pre.shape[2]
    held = pl.BlockSpec(memory_space=pl.ANY)
    vmem = pl.BlockSpec(memory_space=pltpu.VMEM)
    wide, tall = (rows, hid), (hid, width // 2)
    return pl.pallas_call(
        functools.partial(side_body, turn),
        out_shape=(shape(wide), shape(wide), shape(tall, F32), shape(tall)),
        in_specs=[pl.BlockSpec(memory_space=pltpu.SMEM), vmem, vmem] + [held] * len(before),
        out_specs=(held,) * 4,
        scratch_shapes=[
            pltpu.VMEM(wide, BF16),
            pltpu.VMEM(wide, BF16),
            pltpu.VMEM(wide, BF16),
            pltpu.VMEM(tall, F32),
            pltpu.VMEM(tall, BF16),
            pltpu.SemaphoreType.DMA((4,)),
        ],
        input_output_aliases={3 + i: i for i in range(len(before))},
        compiler_params=pltpu.CompilerParams(vmem_limit_bytes=22 << 20),
        cost_estimate=pl.CostEstimate(
            flops=2 * rows * width * hid, bytes_accessed=11 << 20, transcendentals=0
        ),
    )(core, pre, arrived, *before)


def hidden_body(tile_ref, mine_ref, other_ref, rows_ref, low_ref, high_ref, tile_s):
    half = mine_ref.shape[1]
    size = low_ref.shape[0]
    untile_rows(tile_ref, tile_s, rows_ref)
    for i, out in enumerate((low_ref, high_ref)):
        rows = rows_ref[i * size : (i + 1) * size, :]
        part = lax.dot_general(rows[:, :half], mine_ref[...], NT, preferred_element_type=F32)
        part = part + lax.dot_general(
            rows[:, half:], other_ref[...], NT, preferred_element_type=F32
        )
        out[...] = part.astype(BF16)


def back_body(
    low, low_in, high, high_in, silu_ref, slope_ref, gm_ref, go_ref, um_ref, uo_ref,
    out_ref, gate_s, up_s, tile_s,
):
    size = low.shape[0]
    half = gm_ref.shape[0]
    for i, (here, came) in enumerate(((low, low_in), (high, high_in))):
        at = slice(i * size, (i + 1) * size)
        grad = here[...].astype(F32) + came[...].astype(F32)
        up_s[at, :] = (grad * silu_ref[at, :].astype(F32)).astype(BF16)
        gate_s[at, :] = (grad * slope_ref[at, :].astype(F32)).astype(BF16)
    for i, (g, u) in enumerate(((gm_ref, um_ref), (go_ref, uo_ref))):
        total = lax.dot_general(gate_s[...], g[...], NT, preferred_element_type=F32)
        total = total + lax.dot_general(up_s[...], u[...], NT, preferred_element_type=F32)
        tile_rows(total, tile_s, i * half // LANES)
    out_ref[...] = tile_s[...].reshape(out_ref.shape).astype(BF16)


def combine_body(pick_ref, tile_ref, out_ref, rows_s, tile_s):
    untile_rows(tile_ref, tile_s, rows_s)
    out_ref[...] = lax.dot_general(pick_ref[...], rows_s[...], TN, preferred_element_type=F32)


def swap(value):
    return lax.ppermute(value, "core", [(0, 1), (1, 0)])


def pair(value, mask):
    return lax.ppermute(value, "x", [(i, i ^ mask) for i in range(XS)])


def added(a, b):
    return (a.astype(F32) + b.astype(F32)).astype(BF16)


def shards(
    dy_values, dy_scales, route_expert, gate_weight, saved_pre, w_gate, w_up, w_down, w_scale
):
    core = lax.axis_index("core").astype(jnp.int32)[None]
    experts = lax.axis_size(EXPERT)
    tokens, cols = dy_values.shape[1:]
    rows_dev, _, hid = saved_pre.shape[1:]
    width = 2 * cols
    per = width // LANES
    cap = rows_dev * XS * 2 // experts
    slots = cap // 2
    rows = experts * slots
    tiles = (rows, per, LANES)
    block = (experts, slots * per, LANES)

    mine = vmem_call(dy_body, shape((tokens, cols)), 0, 2, 1 << 20, 1 << 18)(
        dy_values[0], dy_scales[0].T
    )
    other = swap(mine)
    saved_pre, mine = lax.optimization_barrier((saved_pre, mine))
    pre = lax.all_gather(saved_pre[0], SEQ, axis=0, tiled=True)
    pre = with_layout_constraint(pre, Layout((0, 1, 2)))
    pick, gate = vmem_call(
        functools.partial(select_body, experts, slots),
        (shape((rows, tokens)), shape((rows, tokens), F32)),
        1, 2, 4 * rows * experts * tokens, 1 << 20,
    )(core, route_expert[0].T, gate_weight[0].T)
    outgoing = vmem_call(
        dispatch_body,
        shape(tiles),
        0, 4, 2 * rows * tokens * width, 2 << 20,
        scratch=(pltpu.VMEM((rows * per, LANES), F32),),
    )(pick, gate, mine, other)
    outgoing, w_gate, w_up, w_down, w_scale = lax.optimization_barrier(
        (outgoing, w_gate, w_up, w_down, w_scale)
    )
    incoming = lax.all_to_all(outgoing.reshape(block), EXPERT, 0, 0, tiled=True).reshape(tiles)
    scales = w_scale[:, 0]
    down_m = dequant_matrix(w_down[0], scales[2].T)
    down_o = swap(down_m)
    gate_m = dequant_matrix(w_gate[0], scales[0])
    up_m = dequant_matrix(w_up[0], scales[1])
    gate_o = swap(gate_m)
    up_o = swap(up_m)
    pre = lax.dynamic_slice_in_dim(
        pre.reshape(experts, cap, 2, hid), core[0] * slots, slots, axis=1
    )
    pre = pre.reshape(rows, 2, hid).transpose(1, 0, 2)
    incoming, pre, gate_o, up_o = lax.optimization_barrier((incoming, pre, gate_o, up_o))

    half = rows // 2
    arrived, low, high = vmem_call(
        hidden_body,
        (shape((rows, width)), shape((half, hid)), shape((half, hid))),
        0, 3, 2 * rows * width * hid, 4 << 20,
        scratch=(pltpu.VMEM((rows * per, LANES), F32),),
    )(incoming, down_m, down_o)

    side = side_call(0, core, pre, arrived, ())
    low, high, *side = lax.optimization_barrier((low, high, *side))
    low = added(low, pair(low, 1))
    high = added(high, pair(high, 3))
    high, *side = lax.optimization_barrier((high, *side))
    silu, slope, down_mine, down_other = side_call(1, core, pre, arrived, side)
    sent = vmem_call(
        back_body,
        shape(tiles),
        0, 10, 4 * rows * width * hid, 6 << 20,
        scratch=(
            pltpu.VMEM((rows, hid), BF16),
            pltpu.VMEM((rows, hid), BF16),
            pltpu.VMEM((rows * per, LANES), F32),
        ),
        limit=20 << 20,
    )(
        low, pair(low, 3), high, pair(high, 1), silu, slope, gate_m, gate_o, up_m, up_o
    )
    returned = lax.all_to_all(sent.reshape(block), EXPERT, 0, 0, tiled=True).reshape(tiles)

    down_grad = down_mine + swap(down_other).astype(F32)
    down_grad = down_grad.astype(BF16)[None]
    down_grad, returned = lax.optimization_barrier((down_grad, returned))

    combined = vmem_call(
        combine_body,
        shape((tokens, width), F32),
        0, 2, 2 * rows * tokens * width, 2 << 20,
        scratch=(pltpu.VMEM((rows, width), BF16), pltpu.VMEM((rows * per, LANES), F32)),
    )(pick, returned)
    input_grad = combined[:, :cols] + swap(combined[:, cols:])
    return (input_grad.astype(BF16)[None], down_grad)


def solution(mesh):
    fine = Mesh(mesh.devices.reshape(XS, 2, 8, 8), SEQ + EXPERT)
    in_specs = (
        P(EXPERT, None, SEQ),
        P(EXPERT, None, SEQ),
        P(EXPERT, None, None),
        P(EXPERT, None, None),
        P(EXPERT, SEQ, None, None),
        P(EXPERT, SEQ, None),
        P(EXPERT, SEQ, None),
        P(EXPERT, None, SEQ),
        P(None, EXPERT, SEQ, None),
    )
    out_specs = (P(EXPERT, None, SEQ), P(EXPERT, None, SEQ))
    return jax.shard_map(shards, mesh=fine, in_specs=in_specs, out_specs=out_specs, check_vma=False)
```

```python
import functools

import jax
import jax.numpy as jnp
from jax import lax
from jax.experimental import pallas as pl
from jax.experimental.layout import Layout, with_layout_constraint
from jax.experimental.pallas import tpu as pltpu
from jax.sharding import Mesh
from jax.sharding import PartitionSpec as P

EXPERT = ("z", "y")
SEQ = ("x", "core")
XS = 4
LANES = 128
HIGHEST = lax.Precision.HIGHEST
NT = (((1,), (1,)), ((), ()))
TN = (((0,), (0,)), ((), ()))
F32 = jnp.float32
BF16 = jnp.bfloat16


def vmem_call(body, out_shape, n_smem, n_in, flops, nbytes, scratch=(), limit=16 << 20):
    smem = pl.BlockSpec(memory_space=pltpu.SMEM)
    vmem = pl.BlockSpec(memory_space=pltpu.VMEM)
    outs = jax.tree.map(lambda _: vmem, out_shape)
    return pl.pallas_call(
        body,
        out_shape=out_shape,
        in_specs=[smem] * n_smem + [vmem] * n_in,
        out_specs=outs,
        scratch_shapes=list(scratch),
        compiler_params=pltpu.CompilerParams(vmem_limit_bytes=limit),
        cost_estimate=pl.CostEstimate(flops=flops, bytes_accessed=nbytes, transcendentals=0),
    )


def shape(dims, dtype=BF16):
    return jax.ShapeDtypeStruct(dims, dtype)


def dequant_matrix(values, scales):
    rows_in, cols_in = values.shape
    row_blocks, col_blocks = scales.shape
    grid = values.astype(F32).reshape(
        row_blocks, rows_in // row_blocks, col_blocks, cols_in // col_blocks
    )
    return (grid * scales[:, None, :, None]).reshape(rows_in, cols_in).astype(BF16)


def iota(dims, axis):
    return lax.broadcasted_iota(jnp.int32, dims, axis)


def onehot(condition, dtype=BF16):
    return jnp.where(condition, 1.0, 0.0).astype(dtype)


def dy_body(value_ref, scale_ref, out_ref):
    blocks, cols = scale_ref.shape[0], value_ref.shape[1]
    first = iota((blocks, cols), 0) * (cols // blocks)
    lane = iota((blocks, cols), 1)
    spread = onehot((lane >= first) & (lane < first + cols // blocks), F32)
    scale = lax.dot_general(
        scale_ref[...], spread, TN, precision=HIGHEST, preferred_element_type=F32
    )
    out_ref[...] = (value_ref[...].astype(F32) * scale).astype(BF16)


def select_body(experts, slots, core_ref, route_ref, weight_ref, pick_ref, gate_ref):
    top, tokens = route_ref.shape
    rows = experts * slots
    label = iota((experts, tokens), 0)
    named = jnp.zeros((experts, tokens), F32)
    weight = jnp.zeros((experts, tokens), F32)
    for k in range(top):
        hit = route_ref[k : k + 1, :] == label
        named = named + jnp.where(hit, 1.0, 0.0)
        weight = weight + jnp.where(hit, weight_ref[k : k + 1, :], 0.0)
    before = onehot(iota((tokens, tokens), 0) < iota((tokens, tokens), 1))
    earlier = jnp.dot(named.astype(BF16), before, preferred_element_type=F32)
    slot = jnp.where(named > 0.0, earlier, -1.0)
    row = iota((rows, experts), 0)
    first = iota((rows, experts), 1) * slots
    spread = (row >= first) & (row < first + slots)
    slot_row = jnp.dot(onehot(spread), slot.astype(BF16), preferred_element_type=F32)
    weight_row = jnp.dot(
        onehot(spread, F32), weight, precision=HIGHEST, preferred_element_type=F32
    )
    place = iota((rows, tokens), 0).astype(F32)
    place = place - slots * jnp.floor((place + 0.5) * (1.0 / slots))
    hit = slot_row == place + (core_ref[0] * slots).astype(F32)
    pick_ref[...] = onehot(hit)
    gate = jnp.sum(jnp.where(hit, weight_row, 0.0), axis=1, keepdims=True)
    gate_ref[...] = jnp.broadcast_to(gate, (rows, tokens))


def tile_rows(value, tile_s, at):
    rows = value.shape[0]
    per = tile_s.shape[0] // rows
    for j in range(value.shape[1] // LANES):
        tile_s[pl.ds(at + j, rows, stride=per), :] = value[:, j * LANES : (j + 1) * LANES]


def untile_rows(tile_ref, tile_s, rows_ref):
    rows, per = tile_ref.shape[:2]
    tile_s[...] = tile_ref[...].astype(F32).reshape(rows * per, LANES)
    for j in range(per):
        rows_ref[:, j * LANES : (j + 1) * LANES] = tile_s[pl.ds(j, rows, stride=per), :].astype(
            BF16
        )


def dispatch_body(pick_ref, gate_ref, mine_ref, other_ref, out_ref, tile_s):
    pick = pick_ref[...]
    gate = gate_ref[:, :1]
    for i, half in enumerate((mine_ref, other_ref)):
        rows = jnp.dot(pick, half[...], preferred_element_type=F32) * gate
        tile_rows(rows, tile_s, i * half.shape[1] // LANES)
    out_ref[...] = tile_s[...].reshape(out_ref.shape).astype(BF16)


def side_body(turn, core_ref, pre_ref, rows_ref, *refs):
    outs, (silu_v, slope_v, act_v, mine_v, other_v, sems) = refs[-10:-6], refs[-6:]
    rows = rows_ref.shape[0]
    cols = mine_v.shape[1]
    size = rows // 4

    @pl.when(core_ref[0] == turn)
    def _():
        for at in range(0, rows, size):
            cut = slice(at, at + size)
            gate_pre = pre_ref[0, cut, :].astype(F32)
            up_pre = pre_ref[1, cut, :].astype(F32)
            sig = jax.nn.sigmoid(gate_pre)
            silu = gate_pre * sig
            silu_v[cut, :] = silu.astype(BF16)
            slope_v[cut, :] = (up_pre * sig * (1.0 + gate_pre * (1.0 - sig))).astype(BF16)
            act_v[cut, :] = (silu * up_pre).astype(BF16)
        held = (silu_v, slope_v, mine_v, other_v)
        stores = [
            pltpu.make_async_copy(src, dst, sems.at[i])
            for i, (src, dst) in enumerate(zip(held, outs))
        ]
        stores[0].start()
        stores[1].start()
        mine_v[...] = lax.dot_general(
            act_v[...], rows_ref[:, :cols], TN, preferred_element_type=F32
        )
        stores[2].start()
        other_v[...] = lax.dot_general(
            act_v[...], rows_ref[:, cols:], TN, preferred_element_type=F32
        ).astype(BF16)
        stores[3].start()
        for store in stores:
            store.wait()


def side_call(turn, core, pre, arrived, before):
    rows, width = arrived.shape
    hid = pre.shape[2]
    held = pl.BlockSpec(memory_space=pl.ANY)
    vmem = pl.BlockSpec(memory_space=pltpu.VMEM)
    wide, tall = (rows, hid), (hid, width // 2)
    return pl.pallas_call(
        functools.partial(side_body, turn),
        out_shape=(shape(wide), shape(wide), shape(tall, F32), shape(tall)),
        in_specs=[pl.BlockSpec(memory_space=pltpu.SMEM), vmem, vmem] + [held] * len(before),
        out_specs=(held,) * 4,
        scratch_shapes=[
            pltpu.VMEM(wide, BF16),
            pltpu.VMEM(wide, BF16),
            pltpu.VMEM(wide, BF16),
            pltpu.VMEM(tall, F32),
            pltpu.VMEM(tall, BF16),
            pltpu.SemaphoreType.DMA((4,)),
        ],
        input_output_aliases={3 + i: i for i in range(len(before))},
        compiler_params=pltpu.CompilerParams(vmem_limit_bytes=22 << 20),
        cost_estimate=pl.CostEstimate(
            flops=2 * rows * width * hid, bytes_accessed=11 << 20, transcendentals=0
        ),
    )(core, pre, arrived, *before)


def hidden_body(tile_ref, mine_ref, other_ref, rows_ref, low_ref, high_ref, tile_s):
    half = mine_ref.shape[1]
    size = low_ref.shape[0]
    untile_rows(tile_ref, tile_s, rows_ref)
    for i, out in enumerate((low_ref, high_ref)):
        rows = rows_ref[i * size : (i + 1) * size, :]
        part = lax.dot_general(rows[:, :half], mine_ref[...], NT, preferred_element_type=F32)
        part = part + lax.dot_general(
            rows[:, half:], other_ref[...], NT, preferred_element_type=F32
        )
        out[...] = part.astype(BF16)


def back_body(
    low, low_in, high, high_in, silu_ref, slope_ref, gm_ref, go_ref, um_ref, uo_ref,
    out_ref, gate_s, up_s, tile_s,
):
    size = low.shape[0]
    half = gm_ref.shape[0]
    for i, (here, came) in enumerate(((low, low_in), (high, high_in))):
        at = slice(i * size, (i + 1) * size)
        grad = here[...].astype(F32) + came[...].astype(F32)
        up_s[at, :] = (grad * silu_ref[at, :].astype(F32)).astype(BF16)
        gate_s[at, :] = (grad * slope_ref[at, :].astype(F32)).astype(BF16)
    for i, (g, u) in enumerate(((gm_ref, um_ref), (go_ref, uo_ref))):
        total = lax.dot_general(gate_s[...], g[...], NT, preferred_element_type=F32)
        total = total + lax.dot_general(up_s[...], u[...], NT, preferred_element_type=F32)
        tile_rows(total, tile_s, i * half // LANES)
    out_ref[...] = tile_s[...].reshape(out_ref.shape).astype(BF16)


def combine_body(pick_ref, tile_ref, out_ref, rows_s, tile_s):
    untile_rows(tile_ref, tile_s, rows_s)
    out_ref[...] = lax.dot_general(pick_ref[...], rows_s[...], TN, preferred_element_type=F32)


def swap(value):
    return lax.ppermute(value, "core", [(0, 1), (1, 0)])


def pair(value, mask):
    return lax.ppermute(value, "x", [(i, i ^ mask) for i in range(XS)])


def added(a, b):
    return (a.astype(F32) + b.astype(F32)).astype(BF16)


def shards(
    dy_values, dy_scales, route_expert, gate_weight, saved_pre, w_gate, w_up, w_down, w_scale
):
    core = lax.axis_index("core").astype(jnp.int32)[None]
    experts = lax.axis_size(EXPERT)
    tokens, cols = dy_values.shape[1:]
    rows_dev, _, hid = saved_pre.shape[1:]
    width = 2 * cols
    per = width // LANES
    cap = rows_dev * XS * 2 // experts
    slots = cap // 2
    rows = experts * slots
    tiles = (rows, per, LANES)
    block = (experts, slots * per, LANES)

    mine = vmem_call(dy_body, shape((tokens, cols)), 0, 2, 1 << 20, 1 << 18)(
        dy_values[0], dy_scales[0].T
    )
    other = swap(mine)
    saved_pre, mine = lax.optimization_barrier((saved_pre, mine))
    pre = lax.all_gather(saved_pre[0], SEQ, axis=0, tiled=True)
    pre = with_layout_constraint(pre, Layout((0, 1, 2)))
    pick, gate = vmem_call(
        functools.partial(select_body, experts, slots),
        (shape((rows, tokens)), shape((rows, tokens), F32)),
        1, 2, 4 * rows * experts * tokens, 1 << 20,
    )(core, route_expert[0].T, gate_weight[0].T)
    outgoing = vmem_call(
        dispatch_body,
        shape(tiles),
        0, 4, 2 * rows * tokens * width, 2 << 20,
        scratch=(pltpu.VMEM((rows * per, LANES), F32),),
    )(pick, gate, mine, other)
    outgoing, w_gate, w_up, w_down, w_scale = lax.optimization_barrier(
        (outgoing, w_gate, w_up, w_down, w_scale)
    )
    incoming = lax.all_to_all(outgoing.reshape(block), EXPERT, 0, 0, tiled=True).reshape(tiles)
    scales = w_scale[:, 0]
    gate_m = dequant_matrix(w_gate[0], scales[0])
    up_m = dequant_matrix(w_up[0], scales[1])
    gate_o = swap(gate_m)
    up_o = swap(up_m)
    gate_o, up_o, w_down = lax.optimization_barrier((gate_o, up_o, w_down))
    down_m = dequant_matrix(w_down[0], scales[2].T)
    down_o = swap(down_m)
    pre = lax.dynamic_slice_in_dim(
        pre.reshape(experts, cap, 2, hid), core[0] * slots, slots, axis=1
    )
    pre = pre.reshape(rows, 2, hid).transpose(1, 0, 2)
    incoming, pre, gate_o, up_o = lax.optimization_barrier((incoming, pre, gate_o, up_o))

    half = rows // 2
    arrived, low, high = vmem_call(
        hidden_body,
        (shape((rows, width)), shape((half, hid)), shape((half, hid))),
        0, 3, 2 * rows * width * hid, 4 << 20,
        scratch=(pltpu.VMEM((rows * per, LANES), F32),),
    )(incoming, down_m, down_o)

    side = side_call(0, core, pre, arrived, ())
    low, high, *side = lax.optimization_barrier((low, high, *side))
    low = added(low, pair(low, 1))
    high = added(high, pair(high, 3))
    high, *side = lax.optimization_barrier((high, *side))
    silu, slope, down_mine, down_other = side_call(1, core, pre, arrived, side)
    sent = vmem_call(
        back_body,
        shape(tiles),
        0, 10, 4 * rows * width * hid, 6 << 20,
        scratch=(
            pltpu.VMEM((rows, hid), BF16),
            pltpu.VMEM((rows, hid), BF16),
            pltpu.VMEM((rows * per, LANES), F32),
        ),
        limit=20 << 20,
    )(
        low, pair(low, 3), high, pair(high, 1), silu, slope, gate_m, gate_o, up_m, up_o
    )
    returned = lax.all_to_all(sent.reshape(block), EXPERT, 0, 0, tiled=True).reshape(tiles)

    down_grad = down_mine + swap(down_other).astype(F32)
    down_grad = down_grad.astype(BF16)[None]
    down_grad, returned = lax.optimization_barrier((down_grad, returned))

    combined = vmem_call(
        combine_body,
        shape((tokens, width), F32),
        0, 2, 2 * rows * tokens * width, 2 << 20,
        scratch=(pltpu.VMEM((rows, width), BF16), pltpu.VMEM((rows * per, LANES), F32)),
    )(pick, returned)
    input_grad = combined[:, :cols] + swap(combined[:, cols:])
    return (input_grad.astype(BF16)[None], down_grad)


def solution(mesh):
    fine = Mesh(mesh.devices.reshape(XS, 2, 8, 8), SEQ + EXPERT)
    in_specs = (
        P(EXPERT, None, SEQ),
        P(EXPERT, None, SEQ),
        P(EXPERT, None, None),
        P(EXPERT, None, None),
        P(EXPERT, SEQ, None, None),
        P(EXPERT, SEQ, None),
        P(EXPERT, SEQ, None),
        P(EXPERT, None, SEQ),
        P(None, EXPERT, SEQ, None),
    )
    out_specs = (P(EXPERT, None, SEQ), P(EXPERT, None, SEQ))
    return jax.shard_map(shards, mesh=fine, in_specs=in_specs, out_specs=out_specs, check_vma=False)
```

```python
import functools

import jax
import jax.numpy as jnp
from jax import lax
from jax.experimental import pallas as pl
from jax.experimental.layout import Layout, with_layout_constraint
from jax.experimental.pallas import tpu as pltpu
from jax.sharding import Mesh
from jax.sharding import PartitionSpec as P

EXPERT = ("z", "y")
SEQ = ("x", "core")
XS = 4
LANES = 128
HIGHEST = lax.Precision.HIGHEST
NT = (((1,), (1,)), ((), ()))
TN = (((0,), (0,)), ((), ()))
F32 = jnp.float32
BF16 = jnp.bfloat16


def vmem_call(body, out_shape, n_smem, n_in, flops, nbytes, scratch=(), limit=16 << 20):
    smem = pl.BlockSpec(memory_space=pltpu.SMEM)
    vmem = pl.BlockSpec(memory_space=pltpu.VMEM)
    outs = jax.tree.map(lambda _: vmem, out_shape)
    return pl.pallas_call(
        body,
        out_shape=out_shape,
        in_specs=[smem] * n_smem + [vmem] * n_in,
        out_specs=outs,
        scratch_shapes=list(scratch),
        compiler_params=pltpu.CompilerParams(vmem_limit_bytes=limit),
        cost_estimate=pl.CostEstimate(flops=flops, bytes_accessed=nbytes, transcendentals=0),
    )


def shape(dims, dtype=BF16):
    return jax.ShapeDtypeStruct(dims, dtype)


def dequant_matrix(values, scales):
    rows_in, cols_in = values.shape
    row_blocks, col_blocks = scales.shape
    grid = values.astype(F32).reshape(
        row_blocks, rows_in // row_blocks, col_blocks, cols_in // col_blocks
    )
    return (grid * scales[:, None, :, None]).reshape(rows_in, cols_in).astype(BF16)


def iota(dims, axis):
    return lax.broadcasted_iota(jnp.int32, dims, axis)


def onehot(condition, dtype=BF16):
    return jnp.where(condition, 1.0, 0.0).astype(dtype)


def dy_body(value_ref, scale_ref, out_ref):
    blocks, cols = scale_ref.shape[0], value_ref.shape[1]
    first = iota((blocks, cols), 0) * (cols // blocks)
    lane = iota((blocks, cols), 1)
    spread = onehot((lane >= first) & (lane < first + cols // blocks), F32)
    scale = lax.dot_general(
        scale_ref[...], spread, TN, precision=HIGHEST, preferred_element_type=F32
    )
    out_ref[...] = (value_ref[...].astype(F32) * scale).astype(BF16)


def select_body(experts, slots, core_ref, route_ref, weight_ref, pick_ref, gate_ref):
    top, tokens = route_ref.shape
    rows = experts * slots
    label = iota((experts, tokens), 0)
    named = jnp.zeros((experts, tokens), F32)
    weight = jnp.zeros((experts, tokens), F32)
    for k in range(top):
        hit = route_ref[k : k + 1, :] == label
        named = named + jnp.where(hit, 1.0, 0.0)
        weight = weight + jnp.where(hit, weight_ref[k : k + 1, :], 0.0)
    before = onehot(iota((tokens, tokens), 0) < iota((tokens, tokens), 1))
    earlier = jnp.dot(named.astype(BF16), before, preferred_element_type=F32)
    slot = jnp.where(named > 0.0, earlier, -1.0)
    row = iota((rows, experts), 0)
    first = iota((rows, experts), 1) * slots
    spread = (row >= first) & (row < first + slots)
    slot_row = jnp.dot(onehot(spread), slot.astype(BF16), preferred_element_type=F32)
    weight_row = jnp.dot(
        onehot(spread, F32), weight, precision=HIGHEST, preferred_element_type=F32
    )
    place = iota((rows, tokens), 0).astype(F32)
    place = place - slots * jnp.floor((place + 0.5) * (1.0 / slots))
    hit = slot_row == place + (core_ref[0] * slots).astype(F32)
    pick_ref[...] = onehot(hit)
    gate = jnp.sum(jnp.where(hit, weight_row, 0.0), axis=1, keepdims=True)
    gate_ref[...] = jnp.broadcast_to(gate, (rows, tokens))


def tile_rows(value, tile_s, at):
    rows = value.shape[0]
    per = tile_s.shape[0] // rows
    for j in range(value.shape[1] // LANES):
        tile_s[pl.ds(at + j, rows, stride=per), :] = value[:, j * LANES : (j + 1) * LANES]


def untile_rows(tile_ref, tile_s, rows_ref):
    rows, per = tile_ref.shape[:2]
    tile_s[...] = tile_ref[...].astype(F32).reshape(rows * per, LANES)
    for j in range(per):
        rows_ref[:, j * LANES : (j + 1) * LANES] = tile_s[pl.ds(j, rows, stride=per), :].astype(
            BF16
        )


def dispatch_body(pick_ref, gate_ref, mine_ref, other_ref, out_ref, tile_s):
    pick = pick_ref[...]
    gate = gate_ref[:, :1]
    for i, half in enumerate((mine_ref, other_ref)):
        rows = jnp.dot(pick, half[...], preferred_element_type=F32) * gate
        tile_rows(rows, tile_s, i * half.shape[1] // LANES)
    out_ref[...] = tile_s[...].reshape(out_ref.shape).astype(BF16)


def side_body(turn, core_ref, pre_ref, rows_ref, *refs):
    outs, (silu_v, slope_v, act_v, mine_v, other_v, sems) = refs[-10:-6], refs[-6:]
    rows = rows_ref.shape[0]
    cols = mine_v.shape[1]
    size = rows // 4

    @pl.when(core_ref[0] == turn)
    def _():
        for at in range(0, rows, size):
            cut = slice(at, at + size)
            gate_pre = pre_ref[0, cut, :].astype(F32)
            up_pre = pre_ref[1, cut, :].astype(F32)
            sig = jax.nn.sigmoid(gate_pre)
            silu = gate_pre * sig
            silu_v[cut, :] = silu.astype(BF16)
            slope_v[cut, :] = (up_pre * sig * (1.0 + gate_pre * (1.0 - sig))).astype(BF16)
            act_v[cut, :] = (silu * up_pre).astype(BF16)
        held = (silu_v, slope_v, mine_v, other_v)
        stores = [
            pltpu.make_async_copy(src, dst, sems.at[i])
            for i, (src, dst) in enumerate(zip(held, outs))
        ]
        stores[0].start()
        stores[1].start()
        mine_v[...] = lax.dot_general(
            act_v[...], rows_ref[:, :cols], TN, preferred_element_type=F32
        )
        stores[2].start()
        other_v[...] = lax.dot_general(
            act_v[...], rows_ref[:, cols:], TN, preferred_element_type=F32
        ).astype(BF16)
        stores[3].start()
        for store in stores:
            store.wait()


def side_call(turn, core, pre, arrived, before):
    rows, width = arrived.shape
    hid = pre.shape[2]
    held = pl.BlockSpec(memory_space=pl.ANY)
    vmem = pl.BlockSpec(memory_space=pltpu.VMEM)
    wide, tall = (rows, hid), (hid, width // 2)
    return pl.pallas_call(
        functools.partial(side_body, turn),
        out_shape=(shape(wide), shape(wide), shape(tall, F32), shape(tall)),
        in_specs=[pl.BlockSpec(memory_space=pltpu.SMEM), vmem, vmem] + [held] * len(before),
        out_specs=(held,) * 4,
        scratch_shapes=[
            pltpu.VMEM(wide, BF16),
            pltpu.VMEM(wide, BF16),
            pltpu.VMEM(wide, BF16),
            pltpu.VMEM(tall, F32),
            pltpu.VMEM(tall, BF16),
            pltpu.SemaphoreType.DMA((4,)),
        ],
        input_output_aliases={3 + i: i for i in range(len(before))},
        compiler_params=pltpu.CompilerParams(vmem_limit_bytes=22 << 20),
        cost_estimate=pl.CostEstimate(
            flops=2 * rows * width * hid, bytes_accessed=11 << 20, transcendentals=0
        ),
    )(core, pre, arrived, *before)


def hidden_body(tile_ref, mine_ref, other_ref, rows_ref, low_ref, high_ref, tile_s):
    half = mine_ref.shape[1]
    size = low_ref.shape[0]
    untile_rows(tile_ref, tile_s, rows_ref)
    for i, out in enumerate((low_ref, high_ref)):
        rows = rows_ref[i * size : (i + 1) * size, :]
        part = lax.dot_general(rows[:, :half], mine_ref[...], NT, preferred_element_type=F32)
        part = part + lax.dot_general(
            rows[:, half:], other_ref[...], NT, preferred_element_type=F32
        )
        out[...] = part.astype(BF16)


def back_body(
    low, low_in, high, high_in, silu_ref, slope_ref, gm_ref, go_ref, um_ref, uo_ref,
    out_ref, gate_s, up_s, tile_s,
):
    size = low.shape[0]
    half = gm_ref.shape[0]
    for i, (here, came) in enumerate(((low, low_in), (high, high_in))):
        at = slice(i * size, (i + 1) * size)
        grad = here[...].astype(F32) + came[...].astype(F32)
        up_s[at, :] = (grad * silu_ref[at, :].astype(F32)).astype(BF16)
        gate_s[at, :] = (grad * slope_ref[at, :].astype(F32)).astype(BF16)
    for i, (g, u) in enumerate(((gm_ref, um_ref), (go_ref, uo_ref))):
        total = lax.dot_general(gate_s[...], g[...], NT, preferred_element_type=F32)
        total = total + lax.dot_general(up_s[...], u[...], NT, preferred_element_type=F32)
        tile_rows(total, tile_s, i * half // LANES)
    out_ref[...] = tile_s[...].reshape(out_ref.shape).astype(BF16)


def combine_body(pick_ref, tile_ref, mine_ref, other_ref, rows_s, tile_s):
    cols = mine_ref.shape[1]
    untile_rows(tile_ref, tile_s, rows_s)
    total = lax.dot_general(pick_ref[...], rows_s[...], TN, preferred_element_type=F32)
    mine_ref[...] = total[:, :cols]
    other_ref[...] = total[:, cols:].astype(BF16)


def swap(value):
    return lax.ppermute(value, "core", [(0, 1), (1, 0)])


def pair(value, mask):
    return lax.ppermute(value, "x", [(i, i ^ mask) for i in range(XS)])


def added(a, b):
    return (a.astype(F32) + b.astype(F32)).astype(BF16)


def shards(
    dy_values, dy_scales, route_expert, gate_weight, saved_pre, w_gate, w_up, w_down, w_scale
):
    core = lax.axis_index("core").astype(jnp.int32)[None]
    experts = lax.axis_size(EXPERT)
    tokens, cols = dy_values.shape[1:]
    rows_dev, _, hid = saved_pre.shape[1:]
    width = 2 * cols
    per = width // LANES
    cap = rows_dev * XS * 2 // experts
    slots = cap // 2
    rows = experts * slots
    tiles = (rows, per, LANES)
    block = (experts, slots * per, LANES)

    mine = vmem_call(dy_body, shape((tokens, cols)), 0, 2, 1 << 20, 1 << 18)(
        dy_values[0], dy_scales[0].T
    )
    other = swap(mine)
    saved_pre, mine = lax.optimization_barrier((saved_pre, mine))
    pre = lax.all_gather(saved_pre[0], SEQ, axis=0, tiled=True)
    pre = with_layout_constraint(pre, Layout((0, 1, 2)))
    pick, gate = vmem_call(
        functools.partial(select_body, experts, slots),
        (shape((rows, tokens)), shape((rows, tokens), F32)),
        1, 2, 4 * rows * experts * tokens, 1 << 20,
    )(core, route_expert[0].T, gate_weight[0].T)
    outgoing = vmem_call(
        dispatch_body,
        shape(tiles),
        0, 4, 2 * rows * tokens * width, 2 << 20,
        scratch=(pltpu.VMEM((rows * per, LANES), F32),),
    )(pick, gate, mine, other)
    outgoing, w_gate, w_up, w_down, w_scale = lax.optimization_barrier(
        (outgoing, w_gate, w_up, w_down, w_scale)
    )
    incoming = lax.all_to_all(outgoing.reshape(block), EXPERT, 0, 0, tiled=True).reshape(tiles)
    scales = w_scale[:, 0]
    gate_m = dequant_matrix(w_gate[0], scales[0])
    up_m = dequant_matrix(w_up[0], scales[1])
    gate_o = swap(gate_m)
    up_o = swap(up_m)
    gate_o, up_o, w_down = lax.optimization_barrier((gate_o, up_o, w_down))
    down_m = dequant_matrix(w_down[0], scales[2].T)
    down_o = swap(down_m)
    pre = lax.dynamic_slice_in_dim(
        pre.reshape(experts, cap, 2, hid), core[0] * slots, slots, axis=1
    )
    pre = pre.reshape(rows, 2, hid).transpose(1, 0, 2)
    incoming, pre, gate_o, up_o = lax.optimization_barrier((incoming, pre, gate_o, up_o))

    half = rows // 2
    arrived, low, high = vmem_call(
        hidden_body,
        (shape((rows, width)), shape((half, hid)), shape((half, hid))),
        0, 3, 2 * rows * width * hid, 4 << 20,
        scratch=(pltpu.VMEM((rows * per, LANES), F32),),
    )(incoming, down_m, down_o)

    side = side_call(0, core, pre, arrived, ())
    low, high, *side = lax.optimization_barrier((low, high, *side))
    low = added(low, pair(low, 1))
    high = added(high, pair(high, 3))
    high, *side = lax.optimization_barrier((high, *side))
    silu, slope, down_mine, down_other = side_call(1, core, pre, arrived, side)
    sent = vmem_call(
        back_body,
        shape(tiles),
        0, 10, 4 * rows * width * hid, 6 << 20,
        scratch=(
            pltpu.VMEM((rows, hid), BF16),
            pltpu.VMEM((rows, hid), BF16),
            pltpu.VMEM((rows * per, LANES), F32),
        ),
        limit=20 << 20,
    )(
        low, pair(low, 3), high, pair(high, 1), silu, slope, gate_m, gate_o, up_m, up_o
    )
    returned = lax.all_to_all(sent.reshape(block), EXPERT, 0, 0, tiled=True).reshape(tiles)

    down_grad = down_mine + swap(down_other).astype(F32)
    down_grad = down_grad.astype(BF16)[None]
    down_grad, returned = lax.optimization_barrier((down_grad, returned))

    combined, leaving = vmem_call(
        combine_body,
        (shape((tokens, cols), F32), shape((tokens, cols))),
        0, 2, 2 * rows * tokens * width, 2 << 20,
        scratch=(pltpu.VMEM((rows, width), BF16), pltpu.VMEM((rows * per, LANES), F32)),
    )(pick, returned)
    input_grad = combined + swap(leaving).astype(F32)
    return (input_grad.astype(BF16)[None], down_grad)


def solution(mesh):
    fine = Mesh(mesh.devices.reshape(XS, 2, 8, 8), SEQ + EXPERT)
    in_specs = (
        P(EXPERT, None, SEQ),
        P(EXPERT, None, SEQ),
        P(EXPERT, None, None),
        P(EXPERT, None, None),
        P(EXPERT, SEQ, None, None),
        P(EXPERT, SEQ, None),
        P(EXPERT, SEQ, None),
        P(EXPERT, None, SEQ),
        P(None, EXPERT, SEQ, None),
    )
    out_specs = (P(EXPERT, None, SEQ), P(EXPERT, None, SEQ))
    return jax.shard_map(shards, mesh=fine, in_specs=in_specs, out_specs=out_specs, check_vma=False)
```

```python
import functools

import jax
import jax.numpy as jnp
from jax import lax
from jax.experimental import pallas as pl
from jax.experimental.layout import Layout, with_layout_constraint
from jax.experimental.pallas import tpu as pltpu
from jax.sharding import Mesh
from jax.sharding import PartitionSpec as P

EXPERT = ("z", "y")
SEQ = ("x", "core")
XS = 4
LANES = 128
HIGHEST = lax.Precision.HIGHEST
NT = (((1,), (1,)), ((), ()))
TN = (((0,), (0,)), ((), ()))
F32 = jnp.float32
BF16 = jnp.bfloat16


def vmem_call(body, out_shape, n_smem, n_in, flops, nbytes, scratch=(), limit=16 << 20):
    smem = pl.BlockSpec(memory_space=pltpu.SMEM)
    vmem = pl.BlockSpec(memory_space=pltpu.VMEM)
    outs = jax.tree.map(lambda _: vmem, out_shape)
    return pl.pallas_call(
        body,
        out_shape=out_shape,
        in_specs=[smem] * n_smem + [vmem] * n_in,
        out_specs=outs,
        scratch_shapes=list(scratch),
        compiler_params=pltpu.CompilerParams(vmem_limit_bytes=limit),
        cost_estimate=pl.CostEstimate(flops=flops, bytes_accessed=nbytes, transcendentals=0),
    )


def shape(dims, dtype=BF16):
    return jax.ShapeDtypeStruct(dims, dtype)


def dequant_matrix(values, scales):
    rows_in, cols_in = values.shape
    row_blocks, col_blocks = scales.shape
    grid = values.astype(F32).reshape(
        row_blocks, rows_in // row_blocks, col_blocks, cols_in // col_blocks
    )
    return (grid * scales[:, None, :, None]).reshape(rows_in, cols_in).astype(BF16)


def iota(dims, axis):
    return lax.broadcasted_iota(jnp.int32, dims, axis)


def onehot(condition, dtype=BF16):
    return jnp.where(condition, 1.0, 0.0).astype(dtype)


def dy_body(value_ref, scale_ref, out_ref):
    blocks, cols = scale_ref.shape[0], value_ref.shape[1]
    first = iota((blocks, cols), 0) * (cols // blocks)
    lane = iota((blocks, cols), 1)
    spread = onehot((lane >= first) & (lane < first + cols // blocks), F32)
    scale = lax.dot_general(
        scale_ref[...], spread, TN, precision=HIGHEST, preferred_element_type=F32
    )
    out_ref[...] = (value_ref[...].astype(F32) * scale).astype(BF16)


def select_body(experts, slots, core_ref, route_ref, weight_ref, pick_ref, gate_ref):
    top, tokens = route_ref.shape
    rows = experts * slots
    label = iota((experts, tokens), 0)
    named = jnp.zeros((experts, tokens), F32)
    weight = jnp.zeros((experts, tokens), F32)
    for k in range(top):
        hit = route_ref[k : k + 1, :] == label
        named = named + jnp.where(hit, 1.0, 0.0)
        weight = weight + jnp.where(hit, weight_ref[k : k + 1, :], 0.0)
    before = onehot(iota((tokens, tokens), 0) < iota((tokens, tokens), 1))
    earlier = jnp.dot(named.astype(BF16), before, preferred_element_type=F32)
    slot = jnp.where(named > 0.0, earlier, -1.0)
    row = iota((rows, experts), 0)
    first = iota((rows, experts), 1) * slots
    spread = (row >= first) & (row < first + slots)
    slot_row = jnp.dot(onehot(spread), slot.astype(BF16), preferred_element_type=F32)
    weight_row = jnp.dot(
        onehot(spread, F32), weight, precision=HIGHEST, preferred_element_type=F32
    )
    place = iota((rows, tokens), 0).astype(F32)
    place = place - slots * jnp.floor((place + 0.5) * (1.0 / slots))
    hit = slot_row == place + (core_ref[0] * slots).astype(F32)
    pick_ref[...] = onehot(hit)
    gate = jnp.sum(jnp.where(hit, weight_row, 0.0), axis=1, keepdims=True)
    gate_ref[...] = jnp.broadcast_to(gate, (rows, tokens))


def tile_rows(value, tile_s, at):
    rows = value.shape[0]
    per = tile_s.shape[0] // rows
    for j in range(value.shape[1] // LANES):
        tile_s[pl.ds(at + j, rows, stride=per), :] = value[:, j * LANES : (j + 1) * LANES]


def untile_rows(tile_ref, tile_s, rows_ref):
    rows, per = tile_ref.shape[:2]
    tile_s[...] = tile_ref[...].astype(F32).reshape(rows * per, LANES)
    for j in range(per):
        rows_ref[:, j * LANES : (j + 1) * LANES] = tile_s[pl.ds(j, rows, stride=per), :].astype(
            BF16
        )


def dispatch_body(pick_ref, gate_ref, mine_ref, other_ref, out_ref, tile_s):
    pick = pick_ref[...]
    gate = gate_ref[:, :1]
    for i, half in enumerate((mine_ref, other_ref)):
        rows = jnp.dot(pick, half[...], preferred_element_type=F32) * gate
        tile_rows(rows, tile_s, i * half.shape[1] // LANES)
    out_ref[...] = tile_s[...].reshape(out_ref.shape).astype(BF16)


def side_body(turn, core_ref, pre_ref, rows_ref, *refs):
    outs, (silu_v, slope_v, act_v, mine_v, other_v, sems) = refs[-10:-6], refs[-6:]
    rows = rows_ref.shape[0]
    cols = mine_v.shape[1]
    size = rows // 4

    @pl.when(core_ref[0] == turn)
    def _():
        for at in range(0, rows, size):
            cut = slice(at, at + size)
            gate_pre = pre_ref[0, cut, :].astype(F32)
            up_pre = pre_ref[1, cut, :].astype(F32)
            sig = jax.nn.sigmoid(gate_pre)
            silu = gate_pre * sig
            silu_v[cut, :] = silu.astype(BF16)
            slope_v[cut, :] = (up_pre * sig * (1.0 + gate_pre * (1.0 - sig))).astype(BF16)
            act_v[cut, :] = (silu * up_pre).astype(BF16)
        held = (silu_v, slope_v, mine_v, other_v)
        stores = [
            pltpu.make_async_copy(src, dst, sems.at[i])
            for i, (src, dst) in enumerate(zip(held, outs))
        ]
        stores[0].start()
        stores[1].start()
        mine_v[...] = lax.dot_general(
            act_v[...], rows_ref[:, :cols], TN, preferred_element_type=F32
        )
        stores[2].start()
        other_v[...] = lax.dot_general(
            act_v[...], rows_ref[:, cols:], TN, preferred_element_type=F32
        ).astype(BF16)
        stores[3].start()
        for store in stores:
            store.wait()


def side_call(turn, core, pre, arrived, before):
    rows, width = arrived.shape
    hid = pre.shape[2]
    held = pl.BlockSpec(memory_space=pl.ANY)
    vmem = pl.BlockSpec(memory_space=pltpu.VMEM)
    wide, tall = (rows, hid), (hid, width // 2)
    return pl.pallas_call(
        functools.partial(side_body, turn),
        out_shape=(shape(wide), shape(wide), shape(tall, F32), shape(tall)),
        in_specs=[pl.BlockSpec(memory_space=pltpu.SMEM), vmem, vmem] + [held] * len(before),
        out_specs=(held,) * 4,
        scratch_shapes=[
            pltpu.VMEM(wide, BF16),
            pltpu.VMEM(wide, BF16),
            pltpu.VMEM(wide, BF16),
            pltpu.VMEM(tall, F32),
            pltpu.VMEM(tall, BF16),
            pltpu.SemaphoreType.DMA((4,)),
        ],
        input_output_aliases={3 + i: i for i in range(len(before))},
        compiler_params=pltpu.CompilerParams(vmem_limit_bytes=22 << 20),
        cost_estimate=pl.CostEstimate(
            flops=2 * rows * width * hid, bytes_accessed=11 << 20, transcendentals=0
        ),
    )(core, pre, arrived, *before)


def hidden_body(tile_ref, mine_ref, other_ref, rows_ref, low_ref, high_ref, tile_s):
    half = mine_ref.shape[1]
    size = low_ref.shape[0]
    untile_rows(tile_ref, tile_s, rows_ref)
    for i, out in enumerate((low_ref, high_ref)):
        rows = rows_ref[i * size : (i + 1) * size, :]
        part = lax.dot_general(rows[:, :half], mine_ref[...], NT, preferred_element_type=F32)
        part = part + lax.dot_general(
            rows[:, half:], other_ref[...], NT, preferred_element_type=F32
        )
        out[...] = part.astype(BF16)


def back_body(
    low, low_in, high, high_in, silu_ref, slope_ref, gm_ref, go_ref, um_ref, uo_ref,
    out_ref, gate_s, up_s, tile_s,
):
    size = low.shape[0]
    half = gm_ref.shape[0]
    for i, (here, came) in enumerate(((low, low_in), (high, high_in))):
        at = slice(i * size, (i + 1) * size)
        grad = here[...].astype(F32) + came[...].astype(F32)
        up_s[at, :] = (grad * silu_ref[at, :].astype(F32)).astype(BF16)
        gate_s[at, :] = (grad * slope_ref[at, :].astype(F32)).astype(BF16)
    for i, (g, u) in enumerate(((gm_ref, um_ref), (go_ref, uo_ref))):
        total = lax.dot_general(gate_s[...], g[...], NT, preferred_element_type=F32)
        total = total + lax.dot_general(up_s[...], u[...], NT, preferred_element_type=F32)
        tile_rows(total, tile_s, i * half // LANES)
    out_ref[...] = tile_s[...].reshape(out_ref.shape).astype(BF16)


def combine_body(pick_ref, tile_ref, mine_ref, other_ref, rows_s, tile_s):
    cols = mine_ref.shape[1]
    untile_rows(tile_ref, tile_s, rows_s)
    total = lax.dot_general(pick_ref[...], rows_s[...], TN, preferred_element_type=F32)
    mine_ref[...] = total[:, :cols]
    other_ref[...] = total[:, cols:].astype(BF16)


def swap(value):
    return lax.ppermute(value, "core", [(0, 1), (1, 0)])


def pair(value, mask):
    return lax.ppermute(value, "x", [(i, i ^ mask) for i in range(XS)])


def added(a, b):
    return (a.astype(F32) + b.astype(F32)).astype(BF16)


def shards(
    dy_values, dy_scales, route_expert, gate_weight, saved_pre, w_gate, w_up, w_down, w_scale
):
    core = lax.axis_index("core").astype(jnp.int32)[None]
    experts = lax.axis_size(EXPERT)
    tokens, cols = dy_values.shape[1:]
    rows_dev, _, hid = saved_pre.shape[1:]
    width = 2 * cols
    per = width // LANES
    cap = rows_dev * XS * 2 // experts
    slots = cap // 2
    rows = experts * slots
    tiles = (rows, per, LANES)
    block = (experts, slots * per, LANES)

    mine = vmem_call(dy_body, shape((tokens, cols)), 0, 2, 1 << 20, 1 << 18)(
        dy_values[0], dy_scales[0].T
    )
    other = swap(mine)
    saved_pre, mine = lax.optimization_barrier((saved_pre, mine))
    pre = lax.all_gather(saved_pre[0], SEQ, axis=0, tiled=True)
    pre = with_layout_constraint(pre, Layout((0, 1, 2)))
    pick, gate = vmem_call(
        functools.partial(select_body, experts, slots),
        (shape((rows, tokens)), shape((rows, tokens), F32)),
        1, 2, 4 * rows * experts * tokens, 1 << 20,
    )(core, route_expert[0].T, gate_weight[0].T)
    outgoing = vmem_call(
        dispatch_body,
        shape(tiles),
        0, 4, 2 * rows * tokens * width, 2 << 20,
        scratch=(pltpu.VMEM((rows * per, LANES), F32),),
    )(pick, gate, mine, other)
    outgoing, w_gate, w_up, w_down, w_scale = lax.optimization_barrier(
        (outgoing, w_gate, w_up, w_down, w_scale)
    )
    incoming = lax.all_to_all(outgoing.reshape(block), EXPERT, 0, 0, tiled=True).reshape(tiles)
    scales = w_scale[:, 0]
    gate_m = dequant_matrix(w_gate[0], scales[0])
    up_m = dequant_matrix(w_up[0], scales[1])
    gate_o = swap(gate_m)
    up_o = swap(up_m)
    gate_o, up_o, w_down = lax.optimization_barrier((gate_o, up_o, w_down))
    down_m = dequant_matrix(w_down[0], scales[2].T)
    down_o = swap(down_m)
    pre = lax.dynamic_slice_in_dim(
        pre.reshape(experts, cap, 2, hid), core[0] * slots, slots, axis=1
    )
    pre = pre.reshape(rows, 2, hid).transpose(1, 0, 2)
    incoming, pre, gate_o, up_o = lax.optimization_barrier((incoming, pre, gate_o, up_o))

    half = rows // 2
    arrived, low, high = vmem_call(
        hidden_body,
        (shape((rows, width)), shape((half, hid)), shape((half, hid))),
        0, 3, 2 * rows * width * hid, 4 << 20,
        scratch=(pltpu.VMEM((rows * per, LANES), F32),),
    )(incoming, down_m, down_o)

    side = side_call(0, core, pre, arrived, ())
    low, *side = lax.optimization_barrier((low, *side))
    low = added(low, pair(low, 1))
    high = added(high, pair(high, 3))
    high, *side = lax.optimization_barrier((high, *side))
    silu, slope, down_mine, down_other = side_call(1, core, pre, arrived, side)
    sent = vmem_call(
        back_body,
        shape(tiles),
        0, 10, 4 * rows * width * hid, 6 << 20,
        scratch=(
            pltpu.VMEM((rows, hid), BF16),
            pltpu.VMEM((rows, hid), BF16),
            pltpu.VMEM((rows * per, LANES), F32),
        ),
        limit=20 << 20,
    )(
        low, pair(low, 3), high, pair(high, 1), silu, slope, gate_m, gate_o, up_m, up_o
    )
    returned = lax.all_to_all(sent.reshape(block), EXPERT, 0, 0, tiled=True).reshape(tiles)

    down_grad = down_mine + swap(down_other).astype(F32)
    down_grad = down_grad.astype(BF16)[None]
    down_grad, returned = lax.optimization_barrier((down_grad, returned))

    combined, leaving = vmem_call(
        combine_body,
        (shape((tokens, cols), F32), shape((tokens, cols))),
        0, 2, 2 * rows * tokens * width, 2 << 20,
        scratch=(pltpu.VMEM((rows, width), BF16), pltpu.VMEM((rows * per, LANES), F32)),
    )(pick, returned)
    input_grad = combined + swap(leaving).astype(F32)
    return (input_grad.astype(BF16)[None], down_grad)


def solution(mesh):
    fine = Mesh(mesh.devices.reshape(XS, 2, 8, 8), SEQ + EXPERT)
    in_specs = (
        P(EXPERT, None, SEQ),
        P(EXPERT, None, SEQ),
        P(EXPERT, None, None),
        P(EXPERT, None, None),
        P(EXPERT, SEQ, None, None),
        P(EXPERT, SEQ, None),
        P(EXPERT, SEQ, None),
        P(EXPERT, None, SEQ),
        P(None, EXPERT, SEQ, None),
    )
    out_specs = (P(EXPERT, None, SEQ), P(EXPERT, None, SEQ))
    return jax.shard_map(shards, mesh=fine, in_specs=in_specs, out_specs=out_specs, check_vma=False)
```
